32 devices in a mesh: dp: 8 (over z, x), tensor: 4 (over y, core).
Axes of the slice: x: 2, y: 2, z: 4, core: 2. Of those that a mesh axis runs over, the one named last changes fastest.
Arguments:
- tokens: bfloat16 [64, 16384], P('dp', 'tensor'), may hold values from -6 to 6
- clip_act: float32 [16384], P('tensor'), may hold values from 0.5 to 4
- weight: bfloat16 [16384, 49152], P('tensor', 'dp'), may hold values from -0.046875 to 0.046875
- clip_weight: float32 [49152], P('dp'), may hold values from 0.003 to 0.03
- cotangent: bfloat16 [64, 49152], P('tensor', 'dp'), may hold values from -6 to 6
Outputs:
- projected: bfloat16 [64, 49152], P('tensor', 'dp')
- token_grad: bfloat16 [64, 16384], P('dp', 'tensor')
- weight_grad: bfloat16 [16384, 49152], P('tensor', 'dp')
- clip_act_grad: float32 [16384], P('tensor')
- clip_weight_grad: float32 [49152], P('dp')
The draws below stay inside these ranges and needn't reach their ends.
All inputs are finite; a program needn't handle non-finite values.
Results may differ from the reference program's by a relative error of at most 0.009.
Values may be sent and summed in bfloat16 or wider, within the bound.
A program may use at most 192 MiB of HBM per device.

```python
import math
import jax
import jax.numpy as jnp
from jax import lax

D = 16384
FF = 49152
TOKENS = 64


def with_spikes(drawn, stream_key, source, target, parts, factor):
    owner, partner = [(jnp.arange(drawn.shape[dim]) // (drawn.shape[dim] // parts)).reshape([-1 if axis == dim else 1 for axis in range(drawn.ndim)]) for dim in (source, target)]
    chosen = jax.random.permutation(stream_key, parts)[partner]
    strong = (owner == chosen) | (owner == (partner + parts // 2) % parts)
    return jnp.where(strong, factor * drawn, drawn)


def block_levels(key, dims, split, smallest, largest):
    factor_of = 1.0
    for position, blocks in split:
        steps = jax.random.uniform(jax.random.fold_in(jax.random.fold_in(key, 6), position), (blocks,), jnp.float32, smallest / len(split), largest / len(split))
        factor_of = factor_of * jnp.repeat(jnp.exp(steps), dims[position] // blocks).reshape((-1,) + (1,) * (len(dims) - 1 - position))
    return factor_of


def bell_draw(key, extent, spread, limit, cuts=(), kind=jnp.bfloat16):
    entries = spread * jax.random.normal(key, extent, jnp.float32)
    if cuts:
        entries = entries * block_levels(key, extent, cuts, -0.22, 0.18)
    return jnp.clip(entries, -limit, limit).astype(kind)


def bell_draw_with(key, shape, deviation, limit, split, heavy, kind=jnp.bfloat16):
    drawn = deviation * jax.random.normal(key, shape, jnp.float32)
    if split:
        drawn = drawn * block_levels(key, shape, split, -0.22, 0.18)
    return jnp.clip(with_spikes(drawn, jax.random.fold_in(key, 3), *heavy), -limit, limit).astype(kind)


def setup_inputs(seed: int = 0) -> dict:
    splits = jax.random.split(jax.random.key(seed), 6)
    return {
        "tokens": bell_draw(splits[0], (TOKENS, D), 1.0, 6.0, ((0, 8), (1, 4))),
        "clip_act": jnp.clip(jnp.exp(math.log(4.0) - 2.0794415 * jax.random.uniform(splits[1], (D,), jnp.float32) ** block_levels(splits[1], (D,), ((0, 4),), -0.2, 0.2)), 0.5, 4.0),
        "weight": bell_draw(splits[2], (D, FF), D ** -0.5, 0.046875, ((0, 4), (1, 8))),
        "clip_weight": jnp.clip(jnp.exp(math.log(0.03) - 2.3025851 * jax.random.uniform(splits[3], (FF,), jnp.float32) ** block_levels(splits[3], (FF,), ((0, 8),), -0.2, 0.2)), 0.003, 0.03),
        "cotangent": bell_draw_with(splits[4], (TOKENS, FF), 1.0, 6.0, ((0, 4), (1, 8)), (1, 0, 8, 2.0)),
    }


def sylvester(order):
    index = lax.iota(jnp.int32, order)
    joined = jnp.bitwise_and(index[:, None], index[None, :])
    parity = jnp.zeros((order, order), jnp.int32)
    for bit_number in range(max(order.bit_length() - 1, 0)):
        parity = parity + jnp.bitwise_and(jnp.right_shift(joined, bit_number), 1)
    return (1 - 2 * jnp.bitwise_and(parity, 1)).astype(jnp.float32)

def rotate_full(values):
    row_total, width = values.shape
    levels = width.bit_length() - 1
    outer = 2 ** (levels // 2)
    inner = width // outer
    blocks = values.reshape(row_total, outer, inner)
    blocks = jnp.einsum('rab,ac->rcb', blocks, sylvester(outer), precision=lax.Precision.HIGHEST)
    blocks = jnp.einsum('rcb,bd->rcd', blocks, sylvester(inner), precision=lax.Precision.HIGHEST)
    return blocks.reshape(row_total, width) * (1.0 / math.sqrt(width))

def reference(tokens, clip_act, weight, clip_weight, cotangent):
    rotated = rotate_full(tokens.astype(jnp.float32))
    ratio_act = rotated / clip_act
    tanh_act = jnp.tanh(ratio_act)
    quant_act = (clip_act * tanh_act).astype(jnp.bfloat16)
    slope_act = 1.0 - tanh_act * tanh_act
    edge_act = tanh_act - ratio_act * slope_act
    row_total, width = tokens.shape
    hidden = weight.shape[1]
    block_cols = math.gcd(hidden, 1024)
    block_count = hidden // block_cols

    def one_block(carry, block_index):
        first_col = block_index * block_cols
        weight_block = lax.dynamic_slice_in_dim(weight, first_col, block_cols, 1)
        clip_block = lax.dynamic_slice_in_dim(clip_weight, first_col, block_cols, 0)
        grad_block = lax.dynamic_slice_in_dim(cotangent, first_col, block_cols, 1)
        ratio_weight = weight_block.astype(jnp.float32) / clip_block
        tanh_weight = jnp.tanh(ratio_weight)
        quant_weight = (clip_block * tanh_weight).astype(jnp.bfloat16)
        outputs = jnp.dot(quant_act, quant_weight, preferred_element_type=jnp.float32).astype(jnp.bfloat16)
        carry = carry + jnp.dot(grad_block, quant_weight.T, preferred_element_type=jnp.float32)
        weight_prod = jnp.dot(quant_act.T, grad_block, preferred_element_type=jnp.float32)
        slope_weight = 1.0 - tanh_weight * tanh_weight
        weight_grad = (weight_prod * slope_weight).astype(jnp.bfloat16)
        clip_grad = lax.optimization_barrier(jnp.sum(weight_prod * (tanh_weight - ratio_weight * slope_weight), axis=0))
        return (carry, (outputs, weight_grad, clip_grad))
    initial = jnp.zeros((row_total, width), jnp.float32)
    act_prod, stacked = lax.scan(one_block, initial, jnp.arange(block_count, dtype=jnp.int32))
    outputs, weight_grads, clip_grads = stacked
    projected = jnp.transpose(outputs, (1, 0, 2)).reshape(row_total, hidden)
    weight_grad = jnp.transpose(weight_grads, (1, 0, 2)).reshape(width, hidden)
    clip_weight_grad = clip_grads.reshape(hidden)
    clip_act_grad = lax.optimization_barrier(jnp.sum(act_prod * edge_act, axis=0))
    token_grad = rotate_full(act_prod * slope_act).astype(jnp.bfloat16)
    return (projected, token_grad, weight_grad, clip_act_grad, clip_weight_grad)
```

```python
import functools
import math

import jax
import jax.numpy as jnp
import numpy as np
from jax import lax
from jax.experimental import pallas as pl
from jax.experimental.pallas import tpu as pltpu
from jax.sharding import PartitionSpec as P

MESH = pl.DeviceIdType.MESH
F32, BF16 = jnp.float32, jnp.bfloat16
LANES = 128


def hadamard_tile():
    index = np.arange(LANES)
    joined = index[:, None] & index[None, :]
    parity = np.zeros_like(joined)
    for bit in range(7):
        parity ^= (joined >> bit) & 1
    return (1 - 2 * parity).astype(np.float32)


def sign_of(a, b, count):
    total = 0
    for bit in range(count.bit_length() - 1):
        total = total + ((a // 2**bit) % 2) * ((b // 2**bit) % 2)
    return (1 - 2 * (total % 2)).astype(F32)


def local_rotate(values, had):
    rows, width = values.shape
    count = width // LANES
    blocks = [values[:, i * LANES : (i + 1) * LANES] for i in range(count)]
    step = 1
    while step < count:
        mixed = list(blocks)
        for i in range(count):
            if i & step == 0:
                mixed[i] = blocks[i] + blocks[i + step]
                mixed[i + step] = blocks[i] - blocks[i + step]
        blocks = mixed
        step *= 2
    stacked = jnp.concatenate(blocks, axis=0)
    out = jnp.dot(stacked, had, preferred_element_type=F32, precision=lax.Precision.HIGHEST)
    return jnp.concatenate([out[i * rows : (i + 1) * rows] for i in range(count)], axis=1)


def fold(values):
    half = values.shape[1] // 2
    return jnp.concatenate([values[:, :half], values[:, half:]], axis=0)


def unfold(values):
    half = values.shape[0] // 2
    return jnp.concatenate([values[:half], values[half:]], axis=1)


def greet(tn, dn, me_t, me_d):
    barrier = pltpu.get_barrier_semaphore()
    for k in range(1, tn):
        pl.semaphore_signal(
            barrier, inc=1, device_id=(me_d, (me_t + k) % tn), device_id_type=MESH
        )
    for k in range(1, dn):
        pl.semaphore_signal(
            barrier, inc=1, device_id=((me_d + k) % dn, me_t), device_id_type=MESH
        )
    pl.semaphore_wait(barrier, tn + dn - 2)


def start_copy(src, dst, sems, k, device):
    copy = pltpu.make_async_remote_copy(
        src_ref=src,
        dst_ref=dst,
        send_sem=sems.at[0, k],
        recv_sem=sems.at[1, k],
        device_id=device,
        device_id_type=MESH,
    )
    copy.start()
    return copy


def gather_kernel(
    tn, dn, norm,
    tok_ref, clip_ref, cot_ref, had_ref,
    allcot_ref, allact_ref, slope_ref, edge_ref,
    tok_send, tok_buf, act_send, act_buf, cot_buf,
    tok_sems, cot_sems, act_sems,
):
    me_d, me_t = lax.axis_index("dp"), lax.axis_index("tensor")
    mine = tok_ref[...].astype(F32)
    tok_send[...] = fold(mine).astype(BF16)
    greet(tn, dn, me_t, me_d)
    tok_copies, cot_copies, act_copies = [], [], []
    for k in range(1, tn):
        device = (me_d, (me_t + k) % tn)
        tok_copies.append(start_copy(tok_send, tok_buf.at[k - 1], tok_sems, k - 1, device))
    for k in range(1, tn):
        device = (me_d, (me_t + k) % tn)
        cot_copies.append(start_copy(cot_ref, cot_buf.at[me_t], cot_sems, k - 1, device))
    cot_buf[me_t] = cot_ref[...]
    mixed = mine * sign_of(me_t, me_t, tn)
    for k in range(1, tn):
        tok_copies[k - 1].wait()
        sender = (me_t + tn - k) % tn
        mixed = mixed + unfold(tok_buf[k - 1].astype(F32)) * sign_of(me_t, sender, tn)
    rotated = local_rotate(mixed, had_ref[...]) * norm
    clip = clip_ref[...]
    ratio = rotated / clip
    act = jnp.tanh(ratio)
    act_send[...] = fold(clip * act).astype(BF16)
    for k in range(1, dn):
        device = ((me_d + k) % dn, me_t)
        act_copies.append(start_copy(act_send, act_buf.at[me_d], act_sems, k - 1, device))
    act_buf[me_d] = act_send[...]
    slope = 1.0 - act * act
    slope_ref[...] = slope
    edge_ref[...] = act - ratio * slope
    for copy in cot_copies:
        copy.wait()
    group = cot_ref.shape[0]
    for j in range(tn):
        allcot_ref[j * group : (j + 1) * group, :] = cot_buf[j]
    for copy in act_copies:
        copy.wait()
    rows = tok_ref.shape[0]
    for j in range(0, dn, 2):
        pair = [unfold(act_buf[j + i].astype(F32)) for i in range(2)]
        allact_ref[j * rows : (j + 2) * rows, :] = jnp.concatenate(pair, axis=0).astype(BF16)


def weight_kernel(chunk, act_ref, cot_ref, clip_ref, inv_ref, w_ref, grad_ref, actp_ref, proj_ref, csum_ref):
    first = pl.program_id(0) == 0
    depth, width = w_ref.shape

    @pl.when(first)
    def _():
        proj_ref[...] = jnp.zeros_like(proj_ref)
        csum_ref[...] = jnp.zeros_like(csum_ref)

    actp_ref[...] = jnp.zeros_like(actp_ref)
    act = act_ref[...]
    act_t = act.astype(F32).T.astype(BF16)

    def one(c, carry):
        cols = pl.ds(pl.multiple_of(c * chunk, chunk), chunk)
        cot = cot_ref[:, cols]
        prod = jnp.dot(act_t, cot, preferred_element_type=F32)
        ratio = w_ref[:, cols].astype(F32) * inv_ref[:, cols]
        tanh = jnp.tanh(ratio)
        quant = (clip_ref[:, cols] * tanh).astype(BF16)
        proj_ref[:, cols] += jnp.dot(act, quant, preferred_element_type=F32)
        actp_ref[...] += lax.dot_general(
            cot, quant, (((1,), (1,)), ((), ())), preferred_element_type=F32
        )
        grad = prod * (1.0 - tanh * tanh)
        grad_ref[:, cols] = grad.astype(BF16)
        terms = prod * tanh - ratio * grad
        csum_ref[:, cols] += jnp.sum(terms.reshape(depth // 8, 8, chunk), axis=0)
        return carry

    lax.fori_loop(0, width // chunk, one, 0)


def reduce_kernel(
    tn, dn, norm,
    actp_ref, proj_ref, csum_ref, slope_ref, edge_ref, had_ref,
    out_ref, tokg_ref, cag_ref, cwg_ref,
    act_send, act_buf, proj_send, proj_buf, cs_send, cs_buf, rot_send, rot_buf, ca_send, ca_buf,
    act_sems, proj_sems, cs_sems, rot_sems, ca_sems,
):
    me_d, me_t = lax.axis_index("dp"), lax.axis_index("tensor")
    rows = slope_ref.shape[0]
    group = out_ref.shape[0]
    for j in range(dn):
        act_send[j] = fold(actp_ref[j * rows : (j + 1) * rows, :]).astype(BF16)
    greet(tn, dn, me_t, me_d)
    act_copies, proj_copies, cs_copies, rot_copies, ca_copies = [], [], [], [], []
    for k in range(1, dn):
        peer = (me_d + k) % dn
        act_copies.append(
            start_copy(act_send.at[peer], act_buf.at[k - 1], act_sems, k - 1, (peer, me_t))
        )
    for j in range(tn):
        proj_send[j] = proj_ref[j * group : (j + 1) * group, :].astype(BF16)
    for k in range(1, tn):
        peer = (me_t + k) % tn
        proj_copies.append(
            start_copy(proj_send.at[peer], proj_buf.at[k - 1], proj_sems, k - 1, (me_d, peer))
        )
    cs_send[...] = jnp.sum(csum_ref[...], axis=0, keepdims=True)
    cs_buf[me_t] = cs_send[...]
    for k in range(1, tn):
        peer = (me_t + k) % tn
        cs_copies.append(start_copy(cs_send, cs_buf.at[me_t], cs_sems, k - 1, (me_d, peer)))
    total = actp_ref[pl.ds(pl.multiple_of(me_d * rows, rows), rows), :]
    for k in range(1, dn):
        act_copies[k - 1].wait()
        total = total + unfold(act_buf[k - 1].astype(F32))
    ca_send[...] = jnp.sum(total * edge_ref[...], axis=0, keepdims=True)
    mixed = local_rotate(total * slope_ref[...], had_ref[...]) * norm
    rot_send[...] = fold(mixed).astype(BF16)
    for k in range(1, tn):
        peer = (me_t + k) % tn
        rot_copies.append(start_copy(rot_send, rot_buf.at[k - 1], rot_sems, k - 1, (me_d, peer)))
    for k in range(1, dn):
        peer = (me_d + k) % dn
        ca_copies.append(start_copy(ca_send, ca_buf.at[me_d], ca_sems, k - 1, (peer, me_t)))
    ca_buf[me_d] = ca_send[...]
    own = proj_ref[pl.ds(pl.multiple_of(me_t * group, group), group), :]
    for k in range(1, tn):
        proj_copies[k - 1].wait()
        own = own + proj_buf[k - 1].astype(F32)
    out_ref[...] = own.astype(BF16)
    for copy in cs_copies:
        copy.wait()
    weight_sum = cs_buf[0]
    for j in range(1, tn):
        weight_sum = weight_sum + cs_buf[j]
    cwg_ref[...] = weight_sum
    result = mixed * sign_of(me_t, me_t, tn)
    for k in range(1, tn):
        rot_copies[k - 1].wait()
        sender = (me_t + tn - k) % tn
        result = result + unfold(rot_buf[k - 1].astype(F32)) * sign_of(me_t, sender, tn)
    tokg_ref[...] = result.astype(BF16)
    for copy in ca_copies:
        copy.wait()
    act_sum = ca_buf[0]
    for j in range(1, dn):
        act_sum = act_sum + ca_buf[j]
    cag_ref[...] = act_sum


def body(tn, dn, tokens, clip_act, weight, clip_weight, cotangent):
    rows, width = tokens.shape
    group, hidden = cotangent.shape
    all_rows = rows * dn
    norm = 1.0 / math.sqrt(width * tn)
    had = jnp.asarray(hadamard_tile())
    vmem = pl.BlockSpec(memory_space=pltpu.VMEM)
    sems = lambda n: pltpu.SemaphoreType.DMA((2, n))
    folded = (2 * rows, width // 2)
    all_cot, all_act, slope_act, edge_act = pl.pallas_call(
        functools.partial(gather_kernel, tn, dn, norm),
        out_shape=(
            jax.ShapeDtypeStruct((all_rows, hidden), BF16),
            jax.ShapeDtypeStruct((all_rows, width), BF16),
            jax.ShapeDtypeStruct((rows, width), F32),
            jax.ShapeDtypeStruct((rows, width), F32),
        ),
        in_specs=[vmem] * 4,
        out_specs=(vmem,) * 4,
        scratch_shapes=[
            pltpu.VMEM(folded, BF16),
            pltpu.VMEM((tn - 1,) + folded, BF16),
            pltpu.VMEM(folded, BF16),
            pltpu.VMEM((dn,) + folded, BF16),
            pltpu.VMEM((tn, group, hidden), BF16),
            sems(tn - 1), sems(tn - 1), sems(dn - 1),
        ],
        compiler_params=pltpu.CompilerParams(
            collective_id=0, has_side_effects=True, vmem_limit_bytes=48 * 2**20
        ),
        name="gather",
    )(tokens, clip_act.reshape(1, -1), cotangent, had)

    depth = 256
    chunk = next(c for c in (1024, 768, 512, 256, 128) if hidden % c == 0)
    clip_row = clip_weight.reshape(1, -1)
    grad, act_prod, proj, clip_sum = pl.pallas_call(
        functools.partial(weight_kernel, chunk),
        grid=(width // depth,),
        out_shape=(
            jax.ShapeDtypeStruct((width, hidden), BF16),
            jax.ShapeDtypeStruct((all_rows, width), F32),
            jax.ShapeDtypeStruct((all_rows, hidden), F32),
            jax.ShapeDtypeStruct((8, hidden), F32),
        ),
        in_specs=[
            pl.BlockSpec((all_rows, depth), lambda i: (0, i)),
            pl.BlockSpec((all_rows, hidden), lambda i: (0, 0)),
            pl.BlockSpec((1, hidden), lambda i: (0, 0)),
            pl.BlockSpec((1, hidden), lambda i: (0, 0)),
            pl.BlockSpec((depth, hidden), lambda i: (i, 0)),
        ],
        out_specs=(
            pl.BlockSpec((depth, hidden), lambda i: (i, 0)),
            pl.BlockSpec((all_rows, depth), lambda i: (0, i)),
            pl.BlockSpec((all_rows, hidden), lambda i: (0, 0)),
            pl.BlockSpec((8, hidden), lambda i: (0, 0)),
        ),
        compiler_params=pltpu.CompilerParams(vmem_limit_bytes=48 * 2**20),
        name="weights",
    )(all_act, all_cot, clip_row, 1.0 / clip_row, weight)

    projected, token_grad, clip_act_grad, clip_weight_grad = pl.pallas_call(
        functools.partial(reduce_kernel, tn, dn, norm),
        out_shape=(
            jax.ShapeDtypeStruct((group, hidden), BF16),
            jax.ShapeDtypeStruct((rows, width), BF16),
            jax.ShapeDtypeStruct((1, width), F32),
            jax.ShapeDtypeStruct((1, hidden), F32),
        ),
        in_specs=[vmem] * 6,
        out_specs=(vmem,) * 4,
        scratch_shapes=[
            pltpu.VMEM((dn,) + folded, BF16),
            pltpu.VMEM((dn - 1,) + folded, BF16),
            pltpu.VMEM((tn, group, hidden), BF16),
            pltpu.VMEM((tn - 1, group, hidden), BF16),
            pltpu.VMEM((1, hidden), F32),
            pltpu.VMEM((tn, 1, hidden), F32),
            pltpu.VMEM(folded, BF16),
            pltpu.VMEM((tn - 1,) + folded, BF16),
            pltpu.VMEM((1, width), F32),
            pltpu.VMEM((dn, 1, width), F32),
            sems(dn - 1), sems(tn - 1), sems(tn - 1), sems(tn - 1), sems(dn - 1),
        ],
        compiler_params=pltpu.CompilerParams(
            collective_id=1, has_side_effects=True, vmem_limit_bytes=48 * 2**20
        ),
        name="reduce",
    )(act_prod, proj, clip_sum, slope_act, edge_act, had)
    return projected, token_grad, grad, clip_act_grad.reshape(-1), clip_weight_grad.reshape(-1)


def solution(mesh):
    in_specs = (P("dp", "tensor"), P("tensor"), P("tensor", "dp"), P("dp"), P("tensor", "dp"))
    out_specs = (P("tensor", "dp"), P("dp", "tensor"), P("tensor", "dp"), P("tensor"), P("dp"))
    local = functools.partial(body, mesh.shape["tensor"], mesh.shape["dp"])
    return jax.shard_map(local, mesh=mesh, in_specs=in_specs, out_specs=out_specs, check_vma=False)
```

```python
import functools
import math

import jax
import jax.numpy as jnp
import numpy as np
from jax import lax
from jax.experimental import pallas as pl
from jax.experimental.pallas import tpu as pltpu
from jax.sharding import PartitionSpec as P

MESH = pl.DeviceIdType.MESH
F32, BF16 = jnp.float32, jnp.bfloat16
LANES = 128


def hadamard_tile():
    index = np.arange(LANES)
    joined = index[:, None] & index[None, :]
    parity = np.zeros_like(joined)
    for bit in range(7):
        parity ^= (joined >> bit) & 1
    return (1 - 2 * parity).astype(np.float32)


def sign_of(a, b, count):
    total = 0
    for bit in range(count.bit_length() - 1):
        total = total + ((a // 2**bit) % 2) * ((b // 2**bit) % 2)
    return (1 - 2 * (total % 2)).astype(F32)


def local_rotate(values, had):
    rows, width = values.shape
    count = width // LANES
    blocks = [values[:, i * LANES : (i + 1) * LANES] for i in range(count)]
    step = 1
    while step < count:
        mixed = list(blocks)
        for i in range(count):
            if i & step == 0:
                mixed[i] = blocks[i] + blocks[i + step]
                mixed[i + step] = blocks[i] - blocks[i + step]
        blocks = mixed
        step *= 2
    stacked = jnp.concatenate(blocks, axis=0)
    out = jnp.dot(stacked, had, preferred_element_type=F32, precision=lax.Precision.HIGHEST)
    return jnp.concatenate([out[i * rows : (i + 1) * rows] for i in range(count)], axis=1)


def fold(values):
    half = values.shape[1] // 2
    return jnp.concatenate([values[:, :half], values[:, half:]], axis=0)


def unfold(values):
    half = values.shape[0] // 2
    return jnp.concatenate([values[:half], values[half:]], axis=1)


def greet(tn, dn, me_t, me_d):
    barrier = pltpu.get_barrier_semaphore()
    for k in range(1, tn):
        pl.semaphore_signal(
            barrier, inc=1, device_id=(me_d, (me_t + k) % tn), device_id_type=MESH
        )
    for k in range(1, dn):
        pl.semaphore_signal(
            barrier, inc=1, device_id=((me_d + k) % dn, me_t), device_id_type=MESH
        )
    pl.semaphore_wait(barrier, tn + dn - 2)


def start_copy(src, dst, sems, k, device):
    copy = pltpu.make_async_remote_copy(
        src_ref=src,
        dst_ref=dst,
        send_sem=sems.at[0, k],
        recv_sem=sems.at[1, k],
        device_id=device,
        device_id_type=MESH,
    )
    copy.start()
    return copy


def gather_kernel(
    tn, dn, norm,
    tok_ref, clip_ref, cot_ref, had_ref,
    allcot_ref, allact_ref, slope_ref, edge_ref,
    tok_send, tok_buf, act_send, act_buf, cot_buf, tok_own, clip_own, had_own,
    tok_sems, cot_sems, act_sems, own_sems,
):
    me_d, me_t = lax.axis_index("dp"), lax.axis_index("tensor")
    loads = [
        pltpu.make_async_copy(src, dst, own_sems.at[i])
        for i, (src, dst) in enumerate(
            [
                (tok_ref, tok_own),
                (cot_ref, cot_buf.at[me_t]),
                (clip_ref, clip_own),
                (had_ref, had_own),
            ]
        )
    ]
    for load in loads:
        load.start()
    loads[0].wait()
    mine = tok_own[...].astype(F32)
    tok_send[...] = fold(mine).astype(BF16)
    greet(tn, dn, me_t, me_d)
    tok_copies, cot_copies, act_copies = [], [], []
    for k in range(1, tn):
        device = (me_d, (me_t + k) % tn)
        tok_copies.append(start_copy(tok_send, tok_buf.at[k - 1], tok_sems, k - 1, device))
    loads[1].wait()
    for k in range(1, tn):
        device = (me_d, (me_t + k) % tn)
        cot_copies.append(start_copy(cot_buf.at[me_t], cot_buf.at[me_t], cot_sems, k - 1, device))
    loads[2].wait()
    loads[3].wait()
    mixed = mine * sign_of(me_t, me_t, tn)
    for k in range(1, tn):
        tok_copies[k - 1].wait()
        sender = (me_t + tn - k) % tn
        mixed = mixed + unfold(tok_buf[k - 1].astype(F32)) * sign_of(me_t, sender, tn)
    rotated = local_rotate(mixed, had_own[...]) * norm
    clip = clip_own[...]
    ratio = rotated / clip
    act = jnp.tanh(ratio)
    act_send[...] = fold(clip * act).astype(BF16)
    for k in range(1, dn):
        device = ((me_d + k) % dn, me_t)
        act_copies.append(start_copy(act_send, act_buf.at[me_d], act_sems, k - 1, device))
    act_buf[me_d] = act_send[...]
    slope = 1.0 - act * act
    slope_ref[...] = slope
    edge_ref[...] = act - ratio * slope
    for copy in cot_copies:
        copy.wait()
    group = cot_ref.shape[0]
    for j in range(tn):
        allcot_ref[j * group : (j + 1) * group, :] = cot_buf[j]
    for copy in act_copies:
        copy.wait()
    rows = tok_ref.shape[0]
    for j in range(0, dn, 2):
        pair = [unfold(act_buf[j + i].astype(F32)) for i in range(2)]
        allact_ref[j * rows : (j + 2) * rows, :] = jnp.concatenate(pair, axis=0).astype(BF16)


def weight_kernel(
    chunk, piece,
    act_ref, cot_ref, clip_ref, w_ref, grad_ref, actp_ref, proj_ref, csum_ref, quant_ref, inv_ref,
):
    depth, width = w_ref.shape

    @pl.when(pl.program_id(0) == 0)
    def _():
        proj_ref[...] = jnp.zeros_like(proj_ref)
        csum_ref[...] = jnp.zeros_like(csum_ref)
        inv_ref[...] = 1.0 / clip_ref[...]

    actp_ref[...] = jnp.zeros_like(actp_ref)
    act = act_ref[...]
    act_t = act.astype(F32).T.astype(BF16)

    def products(start):
        cols = slice(start, start + chunk)
        quant = quant_ref[:, cols]
        proj_ref[:, cols] += jnp.dot(act, quant, preferred_element_type=F32)
        actp_ref[...] += lax.dot_general(
            cot_ref[:, cols], quant, (((1,), (1,)), ((), ())), preferred_element_type=F32
        )

    for start in range(0, width, chunk):
        for sub in range(start, start + chunk, 256):
            cols = slice(sub, sub + 256)
            prod_all = jnp.dot(act_t, cot_ref[:, cols], preferred_element_type=F32)
            inv = inv_ref[:, cols]
            clip = clip_ref[:, cols]
            total = csum_ref[:, cols]
            for row in range(0, depth, piece):
                rows = slice(row, row + piece)
                prod = prod_all[rows]
                ratio = w_ref[rows, cols].astype(F32) * inv
                tanh = jnp.tanh(ratio)
                quant_ref[rows, cols] = (clip * tanh).astype(BF16)
                grad = prod * (1.0 - tanh * tanh)
                grad_ref[rows, cols] = grad.astype(BF16)
                terms = prod * tanh - ratio * grad
                total = total + jnp.sum(terms.reshape(piece // 8, 8, 256), axis=0)
            csum_ref[:, cols] = total
        if start:
            products(start - chunk)
    products(width - chunk)


def reduce_kernel(
    tn, dn, norm,
    actp_ref, proj_ref, csum_ref, slope_ref, edge_ref, had_ref,
    out_ref, tokg_ref, cag_ref, cwg_ref,
    act_send, act_buf, proj_send, proj_buf, cs_send, cs_buf, rot_send, rot_buf, ca_send, ca_buf,
    act_sems, proj_sems, cs_sems, rot_sems, ca_sems,
):
    me_d, me_t = lax.axis_index("dp"), lax.axis_index("tensor")
    rows = slope_ref.shape[0]
    group = out_ref.shape[0]
    for j in range(dn):
        act_send[j] = fold(actp_ref[j * rows : (j + 1) * rows, :]).astype(BF16)
    greet(tn, dn, me_t, me_d)
    act_copies, proj_copies, cs_copies, rot_copies, ca_copies = [], [], [], [], []
    for k in range(1, dn):
        peer = (me_d + k) % dn
        act_copies.append(
            start_copy(act_send.at[peer], act_buf.at[k - 1], act_sems, k - 1, (peer, me_t))
        )
    for j in range(tn):
        proj_send[j] = proj_ref[j * group : (j + 1) * group, :].astype(BF16)
    for k in range(1, tn):
        peer = (me_t + k) % tn
        proj_copies.append(
            start_copy(proj_send.at[peer], proj_buf.at[k - 1], proj_sems, k - 1, (me_d, peer))
        )
    cs_send[...] = jnp.sum(csum_ref[...], axis=0, keepdims=True)
    cs_buf[me_t] = cs_send[...]
    for k in range(1, tn):
        peer = (me_t + k) % tn
        cs_copies.append(start_copy(cs_send, cs_buf.at[me_t], cs_sems, k - 1, (me_d, peer)))
    total = actp_ref[pl.ds(pl.multiple_of(me_d * rows, rows), rows), :]
    for k in range(1, dn):
        act_copies[k - 1].wait()
        total = total + unfold(act_buf[k - 1].astype(F32))
    ca_send[...] = jnp.sum(total * edge_ref[...], axis=0, keepdims=True)
    mixed = local_rotate(total * slope_ref[...], had_ref[...]) * norm
    rot_send[...] = fold(mixed).astype(BF16)
    for k in range(1, tn):
        peer = (me_t + k) % tn
        rot_copies.append(start_copy(rot_send, rot_buf.at[k - 1], rot_sems, k - 1, (me_d, peer)))
    for k in range(1, dn):
        peer = (me_d + k) % dn
        ca_copies.append(start_copy(ca_send, ca_buf.at[me_d], ca_sems, k - 1, (peer, me_t)))
    ca_buf[me_d] = ca_send[...]
    own = proj_ref[pl.ds(pl.multiple_of(me_t * group, group), group), :]
    for k in range(1, tn):
        proj_copies[k - 1].wait()
        own = own + proj_buf[k - 1].astype(F32)
    out_ref[...] = own.astype(BF16)
    for copy in cs_copies:
        copy.wait()
    weight_sum = cs_buf[0]
    for j in range(1, tn):
        weight_sum = weight_sum + cs_buf[j]
    cwg_ref[...] = weight_sum
    result = mixed * sign_of(me_t, me_t, tn)
    for k in range(1, tn):
        rot_copies[k - 1].wait()
        sender = (me_t + tn - k) % tn
        result = result + unfold(rot_buf[k - 1].astype(F32)) * sign_of(me_t, sender, tn)
    tokg_ref[...] = result.astype(BF16)
    for copy in ca_copies:
        copy.wait()
    act_sum = ca_buf[0]
    for j in range(1, dn):
        act_sum = act_sum + ca_buf[j]
    cag_ref[...] = act_sum


def body(tn, dn, tokens, clip_act, weight, clip_weight, cotangent):
    rows, width = tokens.shape
    group, hidden = cotangent.shape
    all_rows = rows * dn
    norm = 1.0 / math.sqrt(width * tn)
    had = jnp.asarray(hadamard_tile())
    vmem = pl.BlockSpec(memory_space=pltpu.VMEM)
    sems = lambda n: pltpu.SemaphoreType.DMA((2, n))
    folded = (2 * rows, width // 2)
    all_cot, all_act, slope_act, edge_act = pl.pallas_call(
        functools.partial(gather_kernel, tn, dn, norm),
        out_shape=(
            jax.ShapeDtypeStruct((all_rows, hidden), BF16),
            jax.ShapeDtypeStruct((all_rows, width), BF16),
            jax.ShapeDtypeStruct((rows, width), F32),
            jax.ShapeDtypeStruct((rows, width), F32),
        ),
        in_specs=[pl.BlockSpec(memory_space=pl.ANY)] * 4,
        out_specs=(vmem,) * 4,
        scratch_shapes=[
            pltpu.VMEM(folded, BF16),
            pltpu.VMEM((tn - 1,) + folded, BF16),
            pltpu.VMEM(folded, BF16),
            pltpu.VMEM((dn,) + folded, BF16),
            pltpu.VMEM((tn, group, hidden), BF16),
            pltpu.VMEM((rows, width), BF16),
            pltpu.VMEM((1, width), F32),
            pltpu.VMEM((LANES, LANES), F32),
            sems(tn - 1), sems(tn - 1), sems(dn - 1),
            pltpu.SemaphoreType.DMA((4,)),
        ],
        compiler_params=pltpu.CompilerParams(
            collective_id=0, has_side_effects=True, vmem_limit_bytes=62 * 2**20
        ),
        name="gather",
    )(tokens, clip_act.reshape(1, -1), cotangent, had)

    depth = 256
    chunk = next(c for c in (512, 256) if hidden % c == 0)
    clip_row = clip_weight.reshape(1, -1)
    grad, act_prod, proj, clip_sum = pl.pallas_call(
        functools.partial(weight_kernel, chunk, 64),
        grid=(width // depth,),
        out_shape=(
            jax.ShapeDtypeStruct((width, hidden), BF16),
            jax.ShapeDtypeStruct((all_rows, width), F32),
            jax.ShapeDtypeStruct((all_rows, hidden), F32),
            jax.ShapeDtypeStruct((8, hidden), F32),
        ),
        in_specs=[
            pl.BlockSpec((all_rows, depth), lambda i: (0, i)),
            pl.BlockSpec((all_rows, hidden), lambda i: (0, 0)),
            pl.BlockSpec((1, hidden), lambda i: (0, 0)),
            pl.BlockSpec((depth, hidden), lambda i: (i, 0)),
        ],
        out_specs=(
            pl.BlockSpec((depth, hidden), lambda i: (i, 0)),
            pl.BlockSpec((all_rows, depth), lambda i: (0, i)),
            pl.BlockSpec((all_rows, hidden), lambda i: (0, 0)),
            pl.BlockSpec((8, hidden), lambda i: (0, 0)),
        ),
        scratch_shapes=[pltpu.VMEM((depth, hidden), BF16), pltpu.VMEM((1, hidden), F32)],
        compiler_params=pltpu.CompilerParams(vmem_limit_bytes=48 * 2**20),
        name="weights",
    )(all_act, all_cot, clip_row, weight)

    projected, token_grad, clip_act_grad, clip_weight_grad = pl.pallas_call(
        functools.partial(reduce_kernel, tn, dn, norm),
        out_shape=(
            jax.ShapeDtypeStruct((group, hidden), BF16),
            jax.ShapeDtypeStruct((rows, width), BF16),
            jax.ShapeDtypeStruct((1, width), F32),
            jax.ShapeDtypeStruct((1, hidden), F32),
        ),
        in_specs=[vmem] * 6,
        out_specs=(vmem,) * 4,
        scratch_shapes=[
            pltpu.VMEM((dn,) + folded, BF16),
            pltpu.VMEM((dn - 1,) + folded, BF16),
            pltpu.VMEM((tn, group, hidden), BF16),
            pltpu.VMEM((tn - 1, group, hidden), BF16),
            pltpu.VMEM((1, hidden), F32),
            pltpu.VMEM((tn, 1, hidden), F32),
            pltpu.VMEM(folded, BF16),
            pltpu.VMEM((tn - 1,) + folded, BF16),
            pltpu.VMEM((1, width), F32),
            pltpu.VMEM((dn, 1, width), F32),
            sems(dn - 1), sems(tn - 1), sems(tn - 1), sems(tn - 1), sems(dn - 1),
        ],
        compiler_params=pltpu.CompilerParams(
            collective_id=1, has_side_effects=True, vmem_limit_bytes=48 * 2**20
        ),
        name="reduce",
    )(act_prod, proj, clip_sum, slope_act, edge_act, had)
    return projected, token_grad, grad, clip_act_grad.reshape(-1), clip_weight_grad.reshape(-1)


def solution(mesh):
    in_specs = (P("dp", "tensor"), P("tensor"), P("tensor", "dp"), P("dp"), P("tensor", "dp"))
    out_specs = (P("tensor", "dp"), P("dp", "tensor"), P("tensor", "dp"), P("tensor"), P("dp"))
    local = functools.partial(body, mesh.shape["tensor"], mesh.shape["dp"])
    return jax.shard_map(local, mesh=mesh, in_specs=in_specs, out_specs=out_specs, check_vma=False)
```
